32 devices in a mesh: groups: 2 (over y), chan: 4 (over z), win: 2 (over x), sub: 2 (over core).
Axes of the slice: x: 2, y: 2, z: 4, core: 2. Of those that a mesh axis runs over, the one named last changes fastest.
Arguments:
- records: bfloat16 [2048, 1792], P(('groups', 'chan', 'sub'), 'win'), parts along dimension 0, may hold values from -6 to 6
- lag_weights: float32 [65], replicated, may hold values from -4 to 4
- probes: bfloat16 [2048, 64], P(('groups', 'chan', 'sub')), parts along dimension 0, may hold values from -6 to 6
Outputs:
- covariance: bfloat16 [3, 2048, 256], P(None, ('groups', 'chan', 'sub'), 'win'), parts along dimension 1
- subspace: float32 [2048, 64], P(('groups', 'chan', 'sub')), parts along dimension 0
The draws below stay inside these ranges and needn't reach their ends.
There are 2 independent parts, one for each index of `groups`. The reference program is written for one: setup_inputs(seed, part) draws one part's arguments, and reference() takes and returns one part's arrays. A program takes and returns all parts, laid end to end along the dimension named above; an argument that names none is the same for every part. Nothing has to cross between parts.
All inputs are finite; a program needn't handle non-finite values.
Results may differ from the reference program's by a relative error of at most 0.0051.
Values may be sent and summed in bfloat16 or wider, within the bound.
A program may use at most 64 MiB of HBM per device.

```python
import jax
import jax.numpy as jnp
from jax import lax

CB = 256
K = 64
MAXLAG = 32
NLAG = 65
C = 1024
SAMPLES = 1792
DIST = 3


def level_of(rng, shape, shards, low, top_value):
    level = 1.0
    for position, shards_of in shards:
        steps = jax.random.uniform(jax.random.fold_in(jax.random.fold_in(rng, 6), position), (shards_of,), jnp.float32, low / len(shards), top_value / len(shards))
        level = level * jnp.repeat(jnp.exp(steps), shape[position] // shards_of).reshape((-1,) + (1,) * (len(shape) - 1 - position))
    return level


def scatter_about(key, shape, spread, most, shards=(), held_as=jnp.bfloat16):
    level = level_of(key, shape, shards, -0.22, 0.18) if shards else 1.0
    drawn = jax.random.normal(key, shape, jnp.float32) * spread * level
    return jnp.minimum(jnp.maximum(drawn, -most), most).astype(held_as)


def setup_inputs(seed: int = 0, part: int = 0) -> dict:
    key_list = jax.random.split(jax.random.key(seed), 4)
    part_keys = jax.random.split(jax.random.fold_in(key_list[3], part), 4)
    return {
        "records": scatter_about(part_keys[0], (C, SAMPLES), 1.0, 6.0, ((0, 8), (1, 2))),
        "lag_weights": scatter_about(key_list[1], (NLAG,), 1.0, 4.0, (), jnp.float32),
        "probes": scatter_about(part_keys[2], (C, K), 1.0, 6.0, ((0, 8),)),
    }


def filter_lags(padded, weights, width):

    def add_lag(lag_index, running):
        window = lax.dynamic_slice_in_dim(padded, lag_index, width, 1).astype(jnp.float32)
        return running + weights[lag_index] * window
    return lax.fori_loop(0, weights.shape[0], add_lag, jnp.zeros((padded.shape[0], width), jnp.float32))

def reference(records, lag_weights, probes):
    block_count = C // CB
    symmetric = 0.5 * (lag_weights + lag_weights[::-1])
    padded = jnp.pad(records, ((0, 0), (MAXLAG, MAXLAG)))
    filtered = filter_lags(padded, symmetric, SAMPLES).astype(jnp.bfloat16)
    probes_wide = probes.astype(jnp.float32)

    def row_block(block_index):
        chosen_rows = lax.dynamic_slice_in_dim(records, block_index * CB, CB, 0)
        row_sums = lax.dot_general(chosen_rows.astype(jnp.float32), filtered.astype(jnp.float32), (((1,), (1,)), ((), ())), preferred_element_type=jnp.float32) / SAMPLES
        images = jnp.dot(row_sums, probes_wide, precision=lax.Precision.HIGHEST)
        blocks = row_sums.reshape(CB, block_count, CB)
        chosen = ((block_index + jnp.arange(DIST).astype(jnp.int32)) % block_count).astype(jnp.int32)
        stacked = jnp.take(blocks, chosen, axis=1).transpose(1, 0, 2)
        return (stacked.astype(jnp.bfloat16), images)
    stacks, image_blocks = lax.map(row_block, jnp.arange(block_count).astype(jnp.int32))
    covariance = stacks.transpose(1, 0, 2, 3).reshape(DIST, C, CB)
    images = image_blocks.reshape(C, K)
    gram_matrix = lax.dot_general(images, images, (((0,), (0,)), ((), ())), precision=lax.Precision.HIGHEST) / C
    factor = jnp.linalg.cholesky(gram_matrix)
    subspace = lax.linalg.triangular_solve(factor, images, left_side=False, lower=True, transpose_a=True)
    return (covariance, subspace)
```

```python
import functools

import jax
import jax.numpy as jnp
from jax import lax
from jax.experimental import pallas as pl
from jax.experimental.pallas import tpu as pltpu
from jax.sharding import PartitionSpec as P

MESH = pl.DeviceIdType.MESH
MAXLAG = 32
LANES = 128
HIGHEST = lax.Precision.HIGHEST


def dot_rows(a, b, precision=None):
    return lax.dot_general(
        a, b, (((1,), (1,)), ((), ())), precision=precision, preferred_element_type=jnp.float32
    )


def halves(x):
    high = x.astype(jnp.bfloat16)
    return high, (x - high.astype(jnp.float32)).astype(jnp.bfloat16)


def banded(weights):
    count = weights.shape[1]
    start = LANES - MAXLAG
    lag = lax.broadcasted_iota(jnp.int32, (count, 3 * LANES), 0)
    place = lax.broadcasted_iota(jnp.int32, (count, 3 * LANES), 1)
    forward = jnp.where(place == lag + start, 0.5, 0.0)
    backward = jnp.where(place == start + count - 1 - lag, 0.5, 0.0)
    row = jnp.dot(weights, forward + backward, precision=HIGHEST)
    row = jnp.broadcast_to(row, (LANES, 3 * LANES))
    return pltpu.roll(row, 0, 1, stride=1, stride_axis=0)


def inverse_factor(gram):
    k = gram.shape[0]
    rows = lax.broadcasted_iota(jnp.int32, (k, k), 0)
    columns = lax.broadcasted_iota(jnp.int32, (k, k), 1)
    eye = jnp.where(rows == columns, 1.0, 0.0)
    m = jnp.concatenate([gram, eye], axis=1)
    below = lax.broadcasted_iota(jnp.int32, (k, 1), 0)
    for i in range(k - 1):
        column = m[:, i : i + 1]
        factor = jnp.where(below > i, column / m[i : i + 1, i : i + 1], 0.0)
        m = m - factor * m[i : i + 1, :]
    pivots = jnp.sum(m[:, :k] * eye, axis=1, keepdims=True)
    return m[:, k:] / jnp.sqrt(pivots)


def kernel(
    chans, wins, samples,
    r_ref, w_ref, p_ref,
    cov_ref, sub_ref,
    g, pg, ext, filt, part, sendp, recvp, im, ib, gb,
    local_sem, r_send, r_recv, p_send, p_recv, h_send, h_recv,
    c_send, c_recv, i_send, i_recv, g_send, g_recv,
):
    z = lax.axis_index("chan")
    s = lax.axis_index("sub")
    w = lax.axis_index("win")
    rows, width = r_ref.shape
    dist = cov_ref.shape[0]
    part_width = cov_ref.shape[2]
    peers = 2 * chans
    me = z * 2 + s
    other = 1 - s

    barrier = pltpu.get_barrier_semaphore()

    def greet(o, carry):
        t = lax.rem(me + o, peers)
        pl.semaphore_signal(
            barrier, inc=1, device_id={"chan": t // 2, "sub": t % 2}, device_id_type=MESH
        )
        return carry

    lax.fori_loop(1, peers, greet, 0)
    for o in range(1, wins):
        pl.semaphore_signal(
            barrier, inc=1, device_id={"win": lax.rem(w + o, wins)}, device_id_type=MESH
        )
    pl.semaphore_wait(barrier, peers - 1 + wins - 1)

    def rows_of(sub):
        return pl.ds(pl.multiple_of(sub * rows, rows), rows)

    def to(way):
        if way == 2:
            return {"sub": other}
        return {"chan": z + (1 if way == 1 else -1)}

    def copies(j, way, source_r=None, source_p=None):
        place = rows_of(s)
        return [
            pltpu.make_async_remote_copy(
                src_ref=p_ref if source_p is not None else pg.at[j, place],
                dst_ref=pg.at[j, place],
                send_sem=p_send.at[j, way],
                recv_sem=p_recv.at[j, s],
                device_id=to(way),
                device_id_type=MESH,
            ),
            pltpu.make_async_remote_copy(
                src_ref=r_ref if source_r is not None else g.at[j, place],
                dst_ref=g.at[j, place],
                send_sem=r_send.at[j, way],
                recv_sem=r_recv.at[j, s],
                device_id=to(way),
                device_id_type=MESH,
            ),
        ]

    def landed(j, sub):
        place = rows_of(sub)
        for buffer, sends, receives in ((pg, p_send, p_recv), (g, r_send, r_recv)):
            pltpu.make_async_remote_copy(
                src_ref=buffer.at[j, place],
                dst_ref=buffer.at[j, place],
                send_sem=sends.at[j, 2],
                recv_sem=receives.at[j, sub],
                device_id={"sub": other},
                device_id_type=MESH,
            ).wait_recv()

    def halo(up):
        source = pl.ds(width - LANES, LANES) if up else pl.ds(0, LANES)
        target = pl.ds(0, LANES) if up else pl.ds(width + LANES, LANES)
        return pltpu.make_async_remote_copy(
            src_ref=r_ref.at[:, source],
            dst_ref=ext.at[:, target],
            send_sem=h_send.at[int(up)],
            recv_sem=h_recv.at[int(up)],
            device_id={"win": w + (1 if up else -1)},
            device_id_type=MESH,
        )

    def start_all(items):
        for item in items:
            item.start()

    @pl.when(w < wins - 1)
    def _():
        halo(True).start()

    @pl.when(w > 0)
    def _():
        halo(False).start()

    @pl.when(z < chans - 1)
    def _():
        start_all(copies(z, 1, True, True))

    @pl.when(z > 0)
    def _():
        start_all(copies(z, 0, True, True))

    start_all(copies(z, 2, True, True))
    local = [
        pltpu.make_async_copy(p_ref, pg.at[z, rows_of(s)], local_sem.at[0]),
        pltpu.make_async_copy(r_ref, g.at[z, rows_of(s)], local_sem.at[1]),
    ]
    start_all(local)

    @pl.when(w == 0)
    def _():
        ext[:, :LANES] = jnp.zeros((rows, LANES), ext.dtype)

    @pl.when(w == wins - 1)
    def _():
        ext[:, LANES + width :] = jnp.zeros((rows, LANES), ext.dtype)

    ext[:, LANES : LANES + width] = r_ref[...]
    im[...] = jnp.zeros_like(im)
    band_high, band_low = halves(banded(w_ref[...]))

    @pl.when(w > 0)
    def _():
        halo(True).wait_recv()

    @pl.when(w < wins - 1)
    def _():
        halo(False).wait_recv()

    for b in range(width // LANES):
        window = ext[:, b * LANES : (b + 3) * LANES]
        value = dot_rows(window, band_high) + dot_rows(window, band_low)
        filt[:, b * LANES : (b + 1) * LANES] = value.astype(filt.dtype)

    def part_copy(d, o):
        t = lax.rem(w + o, wins)
        return pltpu.make_async_remote_copy(
            src_ref=sendp.at[d, t],
            dst_ref=recvp.at[d, w],
            send_sem=c_send.at[d, t],
            recv_sem=c_recv.at[d, w],
            device_id={"win": t},
            device_id_type=MESH,
        )

    def block(j):
        value = dot_rows(filt[...], g[j])
        d = lax.rem(j - z + chans, chans)
        high, low = halves(value)
        probes = pg[j]
        im[...] += jnp.dot(high, probes, preferred_element_type=jnp.float32) + jnp.dot(
            low, probes, preferred_element_type=jnp.float32
        )

        @pl.when(d < dist)
        def _():
            for t in range(wins):
                piece = value[:, t * part_width : (t + 1) * part_width]
                part[d, t] = piece
                sendp[d, t] = piece.astype(sendp.dtype)
            for o in range(1, wins):
                part_copy(d, o).start()

    for item in local:
        item.wait()
    landed(z, other)
    block(z)

    def hop(h, carry):
        above, below = z + h, z - h

        @pl.when(above < chans)
        def _():
            landed(above, s)

            @pl.when(z > 0)
            def _():
                start_all(copies(above, 0))

            start_all(copies(above, 2))

        @pl.when(below >= 0)
        def _():
            landed(below, s)

            @pl.when(z < chans - 1)
            def _():
                start_all(copies(below, 1))

            start_all(copies(below, 2))

        @pl.when(above < chans)
        def _():
            landed(above, other)
            block(above)

        @pl.when(below >= 0)
        def _():
            landed(below, other)
            block(below)

        return carry

    lax.fori_loop(1, chans, hop, 0)

    ib[w] = im[...]

    def image_copy(o):
        t = lax.rem(w + o, wins)
        return pltpu.make_async_remote_copy(
            src_ref=ib.at[w],
            dst_ref=ib.at[w],
            send_sem=i_send.at[t],
            recv_sem=i_recv.at[w],
            device_id={"win": t},
            device_id_type=MESH,
        )

    def image_landed(o):
        t = lax.rem(w + o, wins)
        return pltpu.make_async_remote_copy(
            src_ref=ib.at[t],
            dst_ref=ib.at[t],
            send_sem=i_send.at[t],
            recv_sem=i_recv.at[t],
            device_id={"win": t},
            device_id_type=MESH,
        )

    for o in range(1, wins):
        image_copy(o).start()
    for o in range(1, wins):
        image_landed(o).wait_recv()
    images = ib[0]
    for t in range(1, wins):
        images = images + ib[t]
    images = images * (1.0 / samples)
    gb[me] = lax.dot_general(
        images, images, (((0,), (0,)), ((), ())), precision=HIGHEST,
        preferred_element_type=jnp.float32,
    )

    def gram_copy(o, slot):
        t = lax.rem(me + o, peers)
        at = t if slot else me
        return pltpu.make_async_remote_copy(
            src_ref=gb.at[at],
            dst_ref=gb.at[at],
            send_sem=g_send.at[t],
            recv_sem=g_recv.at[at],
            device_id={"chan": t // 2, "sub": t % 2},
            device_id_type=MESH,
        )

    def gram_start(o, carry):
        gram_copy(o, False).start()
        return carry

    lax.fori_loop(1, peers, gram_start, 0)

    def finish(d, carry):
        total = part[d, w]
        for o in range(1, wins):
            t = lax.rem(w + o, wins)
            pltpu.make_async_remote_copy(
                src_ref=recvp.at[d, t],
                dst_ref=recvp.at[d, t],
                send_sem=c_send.at[d, t],
                recv_sem=c_recv.at[d, t],
                device_id={"win": t},
                device_id_type=MESH,
            ).wait_recv()
            total = total + recvp[d, t].astype(jnp.float32)
        cov_ref[d] = (total * (1.0 / samples)).astype(cov_ref.dtype)
        return carry

    lax.fori_loop(0, dist, finish, 0)

    def gram_landed(o, carry):
        gram_copy(o, True).wait_recv()
        return carry

    lax.fori_loop(1, peers, gram_landed, 0)
    gram = lax.fori_loop(1, peers, lambda t, total: total + gb[t], gb[0])
    inverse = inverse_factor(gram * (1.0 / (rows * peers)))
    sub_ref[...] = dot_rows(images, inverse, HIGHEST)

    @pl.when(w < wins - 1)
    def _():
        halo(True).wait_send()

    @pl.when(w > 0)
    def _():
        halo(False).wait_send()

    def drain(j, carry):
        @pl.when((j >= z) & (z > 0))
        def _():
            for item in copies(j, 0):
                item.wait_send()

        @pl.when((j <= z) & (z < chans - 1))
        def _():
            for item in copies(j, 1):
                item.wait_send()

        for item in copies(j, 2):
            item.wait_send()
        return carry

    lax.fori_loop(0, chans, drain, 0)

    def drain_parts(d, carry):
        for o in range(1, wins):
            part_copy(d, o).wait_send()
        return carry

    lax.fori_loop(0, dist, drain_parts, 0)
    for o in range(1, wins):
        image_copy(o).wait_send()

    def drain_gram(o, carry):
        gram_copy(o, False).wait_send()
        return carry

    lax.fori_loop(1, peers, drain_gram, 0)


def body(chans, wins, records, lag_weights, probes):
    rows, width = records.shape
    k = probes.shape[1]
    dist = chans // 2 + 1
    part_width = 2 * rows // wins
    dma = pltpu.SemaphoreType.DMA
    return pl.pallas_call(
        functools.partial(kernel, chans, wins, width * wins),
        out_shape=(
            jax.ShapeDtypeStruct((dist, rows, part_width), jnp.bfloat16),
            jax.ShapeDtypeStruct((rows, k), jnp.float32),
        ),
        in_specs=[pl.BlockSpec(memory_space=pltpu.VMEM)] * 3,
        out_specs=(pl.BlockSpec(memory_space=pltpu.VMEM),) * 2,
        scratch_shapes=[
            pltpu.VMEM((chans, 2 * rows, width), jnp.bfloat16),
            pltpu.VMEM((chans, 2 * rows, k), jnp.bfloat16),
            pltpu.VMEM((rows, width + 2 * LANES), jnp.bfloat16),
            pltpu.VMEM((rows, width), jnp.bfloat16),
            pltpu.VMEM((dist, wins, rows, part_width), jnp.float32),
            pltpu.VMEM((dist, wins, rows, part_width), jnp.bfloat16),
            pltpu.VMEM((dist, wins, rows, part_width), jnp.bfloat16),
            pltpu.VMEM((rows, k), jnp.float32),
            pltpu.VMEM((wins, rows, k), jnp.float32),
            pltpu.VMEM((2 * chans, k, k), jnp.float32),
            dma((2,)),
            dma((chans, 3)), dma((chans, 2)),
            dma((chans, 3)), dma((chans, 2)),
            dma((2,)), dma((2,)),
            dma((dist, wins)), dma((dist, wins)),
            dma((wins,)), dma((wins,)),
            dma((2 * chans,)), dma((2 * chans,)),
        ],
        compiler_params=pltpu.CompilerParams(
            collective_id=0, has_side_effects=True, vmem_limit_bytes=48 * 1024 * 1024
        ),
    )(records, lag_weights.reshape(1, -1), probes)


def solution(mesh):
    return jax.shard_map(
        functools.partial(body, mesh.shape["chan"], mesh.shape["win"]),
        mesh=mesh,
        in_specs=(P(("groups", "chan", "sub"), "win"), P(), P(("groups", "chan", "sub"), None)),
        out_specs=(P(None, ("groups", "chan", "sub"), "win"), P(("groups", "chan", "sub"), None)),
        check_vma=False,
    )
```

```python
import functools

import jax
import jax.numpy as jnp
from jax import lax
from jax.experimental import pallas as pl
from jax.experimental.pallas import tpu as pltpu
from jax.sharding import PartitionSpec as P

MESH = pl.DeviceIdType.MESH
MAXLAG = 32
LANES = 128
PIECE = 16
HIGHEST = lax.Precision.HIGHEST


def dot_rows(a, b, precision=None):
    return lax.dot_general(
        a, b, (((1,), (1,)), ((), ())), precision=precision, preferred_element_type=jnp.float32
    )


def halves(x):
    high = x.astype(jnp.bfloat16)
    return high, (x - high.astype(jnp.float32)).astype(jnp.bfloat16)


def banded(weights):
    count = weights.shape[1]
    start = LANES - MAXLAG
    lag = lax.broadcasted_iota(jnp.int32, (count, 3 * LANES), 0)
    place = lax.broadcasted_iota(jnp.int32, (count, 3 * LANES), 1)
    forward = jnp.where(place == lag + start, 0.5, 0.0)
    backward = jnp.where(place == start + count - 1 - lag, 0.5, 0.0)
    row = jnp.dot(weights, forward + backward, precision=HIGHEST)
    row = jnp.broadcast_to(row, (LANES, 3 * LANES))
    return pltpu.roll(row, 0, 1, stride=1, stride_axis=0)


def inverse_factor(gram):
    k = gram.shape[0]
    rows = lax.broadcasted_iota(jnp.int32, (k, k), 0)
    columns = lax.broadcasted_iota(jnp.int32, (k, k), 1)
    eye = jnp.where(rows == columns, 1.0, 0.0)
    m = jnp.concatenate([gram, eye], axis=1)
    below = lax.broadcasted_iota(jnp.int32, (k, 1), 0)
    for i in range(k - 1):
        column = m[:, i : i + 1]
        factor = jnp.where(below > i, column / m[i : i + 1, i : i + 1], 0.0)
        m = m - factor * m[i : i + 1, :]
    pivots = jnp.sum(m[:, :k] * eye, axis=1, keepdims=True)
    return m[:, k:] / jnp.sqrt(pivots)


def kernel(
    chans, wins, samples,
    r_ref, w_ref, p_ref,
    cov_ref, sub_ref,
    g, ext, filt, part, sendp, recvp, zl, zr, zs, ib, gb,
    local_sem, r_send, r_recv, z_send, z_recv, y_send, y_recv, h_send, h_recv,
    c_send, c_recv, i_send, i_recv, g_send, g_recv,
):
    z = lax.axis_index("chan")
    s = lax.axis_index("sub")
    w = lax.axis_index("win")
    rows, width = r_ref.shape
    dist = cov_ref.shape[0]
    part_width = cov_ref.shape[2]
    peers = 2 * chans
    me = z * 2 + s
    other = 1 - s
    half = chans // 2
    pieces = zs.shape[0]
    owners = [((q * chans) // pieces, q % 2) for q in range(pieces)]

    barrier = pltpu.get_barrier_semaphore()

    def greet(o, carry):
        t = lax.rem(me + o, peers)
        pl.semaphore_signal(
            barrier, inc=1, device_id={"chan": t // 2, "sub": t % 2}, device_id_type=MESH
        )
        return carry

    lax.fori_loop(1, peers, greet, 0)
    for o in range(1, wins):
        pl.semaphore_signal(
            barrier, inc=1, device_id={"win": lax.rem(w + o, wins)}, device_id_type=MESH
        )
    moments = lax.dot_general(
        p_ref[...], r_ref[...], (((0,), (0,)), ((), ())), preferred_element_type=jnp.float32
    )
    for q in range(pieces):
        zl[q] = moments[q * PIECE : (q + 1) * PIECE, :].astype(zl.dtype)
    pl.semaphore_wait(barrier, peers - 1 + wins - 1)

    def rows_of(sub):
        return pl.ds(pl.multiple_of(sub * rows, rows), rows)

    def to(way):
        if way == 2:
            return {"sub": other}
        return {"chan": z + (1 if way == 1 else -1)}

    def copy(j, way, own=False):
        place = rows_of(s)
        return pltpu.make_async_remote_copy(
            src_ref=r_ref if own else g.at[j, place],
            dst_ref=g.at[j, place],
            send_sem=r_send.at[j, way],
            recv_sem=r_recv.at[j, s],
            device_id=to(way),
            device_id_type=MESH,
        )

    def goes_down(j):
        return (z > 0) & (j >= z) & (j - z < half)

    def goes_up(j):
        return (z < chans - 1) & (j <= z) & (j + half < chans)

    def used(j):
        return lax.rem(j - z + chans, chans) < dist

    def landed(j, sub):
        place = rows_of(sub)
        pltpu.make_async_remote_copy(
            src_ref=g.at[j, place],
            dst_ref=g.at[j, place],
            send_sem=r_send.at[j, 2],
            recv_sem=r_recv.at[j, sub],
            device_id={"sub": other},
            device_id_type=MESH,
        ).wait_recv()

    def piece_copy(q):
        return pltpu.make_async_remote_copy(
            src_ref=zl.at[q],
            dst_ref=zr.at[me],
            send_sem=z_send.at[q],
            recv_sem=z_recv.at[me],
            device_id={"chan": owners[q][0], "sub": owners[q][1]},
            device_id_type=MESH,
        )

    def owns(q):
        return (z == owners[q][0]) & (s == owners[q][1])

    def peer(o):
        t = lax.rem(me + o, peers)
        return t, {"chan": t // 2, "sub": t % 2}

    def piece_landed(o, carry):
        t, device = peer(o)
        pltpu.make_async_remote_copy(
            src_ref=zr.at[t],
            dst_ref=zr.at[t],
            send_sem=z_send.at[0],
            recv_sem=z_recv.at[t],
            device_id=device,
            device_id_type=MESH,
        ).wait_recv()
        return carry

    def sum_copy(q, o):
        t, device = peer(o)
        return pltpu.make_async_remote_copy(
            src_ref=zs.at[q],
            dst_ref=zs.at[q],
            send_sem=y_send.at[t],
            recv_sem=y_recv.at[q],
            device_id=device,
            device_id_type=MESH,
        )

    def halo(up):
        source = pl.ds(width - LANES, LANES) if up else pl.ds(0, LANES)
        target = pl.ds(0, LANES) if up else pl.ds(width + LANES, LANES)
        return pltpu.make_async_remote_copy(
            src_ref=r_ref.at[:, source],
            dst_ref=ext.at[:, target],
            send_sem=h_send.at[int(up)],
            recv_sem=h_recv.at[int(up)],
            device_id={"win": w + (1 if up else -1)},
            device_id_type=MESH,
        )

    for q in range(pieces):

        @pl.when(jnp.logical_not(owns(q)))
        def _(q=q):
            piece_copy(q).start()

    @pl.when(w < wins - 1)
    def _():
        halo(True).start()

    @pl.when(w > 0)
    def _():
        halo(False).start()

    @pl.when(goes_up(z))
    def _():
        copy(z, 1, True).start()

    @pl.when(goes_down(z))
    def _():
        copy(z, 0, True).start()

    copy(z, 2, True).start()
    local = pltpu.make_async_copy(r_ref, g.at[z, rows_of(s)], local_sem.at[0])
    local.start()

    @pl.when(w == 0)
    def _():
        ext[:, :LANES] = jnp.zeros((rows, LANES), ext.dtype)

    @pl.when(w == wins - 1)
    def _():
        ext[:, LANES + width :] = jnp.zeros((rows, LANES), ext.dtype)

    ext[:, LANES : LANES + width] = r_ref[...]
    band_high, band_low = halves(banded(w_ref[...]))

    @pl.when(w > 0)
    def _():
        halo(True).wait_recv()

    @pl.when(w < wins - 1)
    def _():
        halo(False).wait_recv()

    for b in range(width // LANES):
        window = ext[:, b * LANES : (b + 3) * LANES]
        value = dot_rows(window, band_high) + dot_rows(window, band_low)
        high, low = halves(value)
        filt[0, :, b * LANES : (b + 1) * LANES] = high
        filt[1, :, b * LANES : (b + 1) * LANES] = low

    for q in range(pieces):

        @pl.when(owns(q))
        def _(q=q):
            lax.fori_loop(1, peers, piece_landed, 0)
            zr[me] = zl[q]
            total = lax.fori_loop(
                1, peers, lambda t, run: run + zr[t].astype(jnp.float32),
                zr[0].astype(jnp.float32),
            )
            zs[q] = total.astype(zs.dtype)

            def send(o, carry):
                sum_copy(q, o).start()
                return carry

            lax.fori_loop(1, peers, send, 0)

    def part_copy(d, o):
        t = lax.rem(w + o, wins)
        return pltpu.make_async_remote_copy(
            src_ref=sendp.at[d, t],
            dst_ref=recvp.at[d, w],
            send_sem=c_send.at[d, t],
            recv_sem=c_recv.at[d, w],
            device_id={"win": t},
            device_id_type=MESH,
        )

    def block(j):
        value = dot_rows(filt[0], g[j]) + dot_rows(filt[1], g[j])
        d = lax.rem(j - z + chans, chans)
        for t in range(wins):
            piece = value[:, t * part_width : (t + 1) * part_width]
            part[d, t] = piece
            sendp[d, t] = piece.astype(sendp.dtype)
        for o in range(1, wins):
            part_copy(d, o).start()

    def forward(h):
        above, below = z + h, z - h

        @pl.when((above < chans) & (h <= half))
        def _():
            landed(above, s)

            @pl.when(goes_down(above))
            def _():
                copy(above, 0).start()

            copy(above, 2).start()

        @pl.when((below >= 0) & (below + half < chans))
        def _():
            landed(below, s)

            @pl.when(goes_up(below))
            def _():
                copy(below, 1).start()

            @pl.when(used(below))
            def _():
                copy(below, 2).start()

    def take(h):
        above, below = z + h, z - h

        @pl.when((above < chans) & (h <= half))
        def _():
            landed(above, other)
            block(above)

        @pl.when((below >= 0) & (below + half < chans) & (h >= half))
        def _():
            landed(below, other)
            block(below)

    forward(1)
    for q in range(pieces):

        @pl.when(jnp.logical_not(owns(q)))
        def _(q=q):
            sum_copy(q, 1).wait_recv()

    moments = zs[...].reshape(pieces * PIECE, width)
    ib[w] = dot_rows(filt[0], moments) + dot_rows(filt[1], moments)

    def image_copy(o):
        t = lax.rem(w + o, wins)
        return pltpu.make_async_remote_copy(
            src_ref=ib.at[w],
            dst_ref=ib.at[w],
            send_sem=i_send.at[t],
            recv_sem=i_recv.at[w],
            device_id={"win": t},
            device_id_type=MESH,
        )

    def image_landed(o):
        t = lax.rem(w + o, wins)
        return pltpu.make_async_remote_copy(
            src_ref=ib.at[t],
            dst_ref=ib.at[t],
            send_sem=i_send.at[t],
            recv_sem=i_recv.at[t],
            device_id={"win": t},
            device_id_type=MESH,
        )

    for o in range(1, wins):
        image_copy(o).start()
    local.wait()
    landed(z, other)
    block(z)
    take(1)
    for o in range(1, wins):
        image_landed(o).wait_recv()
    images = ib[0]
    for t in range(1, wins):
        images = images + ib[t]
    images = images * (1.0 / samples)
    gb[me] = lax.dot_general(
        images, images, (((0,), (0,)), ((), ())), precision=HIGHEST,
        preferred_element_type=jnp.float32,
    )

    def gram_copy(o, slot):
        t = lax.rem(me + o, peers)
        at = t if slot else me
        return pltpu.make_async_remote_copy(
            src_ref=gb.at[at],
            dst_ref=gb.at[at],
            send_sem=g_send.at[t],
            recv_sem=g_recv.at[at],
            device_id={"chan": t // 2, "sub": t % 2},
            device_id_type=MESH,
        )

    def gram_start(o, carry):
        gram_copy(o, False).start()
        return carry

    lax.fori_loop(1, peers, gram_start, 0)

    def hop(h, carry):
        forward(h)
        take(h)
        return carry

    lax.fori_loop(2, chans, hop, 0)

    def gram_landed(o, carry):
        gram_copy(o, True).wait_recv()
        return carry

    lax.fori_loop(1, peers, gram_landed, 0)
    gram = lax.fori_loop(1, peers, lambda t, total: total + gb[t], gb[0])
    inverse = inverse_factor(gram * (1.0 / (rows * peers)))
    sub_ref[...] = dot_rows(images, inverse, HIGHEST)

    def finish(d, carry):
        total = part[d, w]
        for o in range(1, wins):
            t = lax.rem(w + o, wins)
            pltpu.make_async_remote_copy(
                src_ref=recvp.at[d, t],
                dst_ref=recvp.at[d, t],
                send_sem=c_send.at[d, t],
                recv_sem=c_recv.at[d, t],
                device_id={"win": t},
                device_id_type=MESH,
            ).wait_recv()
            total = total + recvp[d, t].astype(jnp.float32)
        cov_ref[d] = (total * (1.0 / samples)).astype(cov_ref.dtype)
        return carry

    lax.fori_loop(0, dist, finish, 0)

    @pl.when(w < wins - 1)
    def _():
        halo(True).wait_send()

    @pl.when(w > 0)
    def _():
        halo(False).wait_send()

    for q in range(pieces):

        @pl.when(jnp.logical_not(owns(q)))
        def _(q=q):
            piece_copy(q).wait_send()

        @pl.when(owns(q))
        def _(q=q):
            def sent(o, carry):
                sum_copy(q, o).wait_send()
                return carry

            lax.fori_loop(1, peers, sent, 0)

    def drain(j, carry):
        @pl.when(goes_down(j))
        def _():
            copy(j, 0).wait_send()

        @pl.when(goes_up(j))
        def _():
            copy(j, 1).wait_send()

        @pl.when(used(j))
        def _():
            copy(j, 2).wait_send()

        return carry

    lax.fori_loop(0, chans, drain, 0)

    def drain_parts(d, carry):
        for o in range(1, wins):
            part_copy(d, o).wait_send()
        return carry

    lax.fori_loop(0, dist, drain_parts, 0)
    for o in range(1, wins):
        image_copy(o).wait_send()

    def drain_gram(o, carry):
        gram_copy(o, False).wait_send()
        return carry

    lax.fori_loop(1, peers, drain_gram, 0)


def body(chans, wins, records, lag_weights, probes):
    rows, width = records.shape
    k = probes.shape[1]
    dist = chans // 2 + 1
    part_width = 2 * rows // wins
    dma = pltpu.SemaphoreType.DMA
    return pl.pallas_call(
        functools.partial(kernel, chans, wins, width * wins),
        out_shape=(
            jax.ShapeDtypeStruct((dist, rows, part_width), jnp.bfloat16),
            jax.ShapeDtypeStruct((rows, k), jnp.float32),
        ),
        in_specs=[pl.BlockSpec(memory_space=pltpu.VMEM)] * 3,
        out_specs=(pl.BlockSpec(memory_space=pltpu.VMEM),) * 2,
        scratch_shapes=[
            pltpu.VMEM((chans, 2 * rows, width), jnp.bfloat16),
            pltpu.VMEM((rows, width + 2 * LANES), jnp.bfloat16),
            pltpu.VMEM((2, rows, width), jnp.bfloat16),
            pltpu.VMEM((dist, wins, rows, part_width), jnp.float32),
            pltpu.VMEM((dist, wins, rows, part_width), jnp.bfloat16),
            pltpu.VMEM((dist, wins, rows, part_width), jnp.bfloat16),
            pltpu.VMEM((k // PIECE, PIECE, width), jnp.bfloat16),
            pltpu.VMEM((2 * chans, PIECE, width), jnp.bfloat16),
            pltpu.VMEM((k // PIECE, PIECE, width), jnp.bfloat16),
            pltpu.VMEM((wins, rows, k), jnp.float32),
            pltpu.VMEM((2 * chans, k, k), jnp.float32),
            dma((1,)),
            dma((chans, 3)), dma((chans, 2)),
            dma((k // PIECE,)), dma((2 * chans,)),
            dma((2 * chans,)), dma((k // PIECE,)),
            dma((2,)), dma((2,)),
            dma((dist, wins)), dma((dist, wins)),
            dma((wins,)), dma((wins,)),
            dma((2 * chans,)), dma((2 * chans,)),
        ],
        compiler_params=pltpu.CompilerParams(
            collective_id=0, has_side_effects=True, vmem_limit_bytes=48 * 1024 * 1024
        ),
    )(records, lag_weights.reshape(1, -1), probes)


def solution(mesh):
    return jax.shard_map(
        functools.partial(body, mesh.shape["chan"], mesh.shape["win"]),
        mesh=mesh,
        in_specs=(P(("groups", "chan", "sub"), "win"), P(), P(("groups", "chan", "sub"), None)),
        out_specs=(P(None, ("groups", "chan", "sub"), "win"), P(("groups", "chan", "sub"), None)),
        check_vma=False,
    )
```

```python
import functools

import jax
import jax.numpy as jnp
from jax import lax
from jax.experimental import pallas as pl
from jax.experimental.pallas import tpu as pltpu
from jax.sharding import PartitionSpec as P

MESH = pl.DeviceIdType.MESH
MAXLAG = 32
LANES = 128
PIECE = 16
CHUNKS = 4
HIGHEST = lax.Precision.HIGHEST


def dot_rows(a, b, precision=None):
    return lax.dot_general(
        a, b, (((1,), (1,)), ((), ())), precision=precision, preferred_element_type=jnp.float32
    )


def halves(x):
    high = x.astype(jnp.bfloat16)
    return high, (x - high.astype(jnp.float32)).astype(jnp.bfloat16)


def banded(weights):
    count = weights.shape[1]
    start = LANES - MAXLAG
    lag = lax.broadcasted_iota(jnp.int32, (count, 3 * LANES), 0)
    place = lax.broadcasted_iota(jnp.int32, (count, 3 * LANES), 1)
    forward = jnp.where(place == lag + start, 0.5, 0.0)
    backward = jnp.where(place == start + count - 1 - lag, 0.5, 0.0)
    row = jnp.dot(weights, forward + backward, precision=HIGHEST)
    row = jnp.broadcast_to(row, (LANES, 3 * LANES))
    return pltpu.roll(row, 0, 1, stride=1, stride_axis=0)


def inverse_factor(gram):
    k = gram.shape[0]
    rows = lax.broadcasted_iota(jnp.int32, (k, k), 0)
    columns = lax.broadcasted_iota(jnp.int32, (k, k), 1)
    eye = jnp.where(rows == columns, 1.0, 0.0)
    m = jnp.concatenate([gram, eye], axis=1)
    below = lax.broadcasted_iota(jnp.int32, (k, 1), 0)
    for i in range(k - 1):
        column = m[:, i : i + 1]
        factor = jnp.where(below > i, column / m[i : i + 1, i : i + 1], 0.0)
        m = m - factor * m[i : i + 1, :]
    pivots = jnp.sum(m[:, :k] * eye, axis=1, keepdims=True)
    return m[:, k:] / jnp.sqrt(pivots)


def kernel(
    chans, wins, samples,
    r_ref, w_ref, p_ref,
    cov_ref, sub_ref,
    g, ext, filt, part, sendp, recvp, zl, zr, zs, ib, gb,
    local_sem, r_send, r_recv, z_send, z_recv, y_send, y_recv, h_send, h_recv,
    c_send, c_recv, i_send, i_recv, g_send, g_recv,
):
    z = lax.axis_index("chan")
    s = lax.axis_index("sub")
    w = lax.axis_index("win")
    rows, width = r_ref.shape
    dist = cov_ref.shape[0]
    part_width = cov_ref.shape[2]
    peers = 2 * chans
    me = z * 2 + s
    other = 1 - s
    half = chans // 2
    pieces = zs.shape[0]
    owners = [((q * chans) // pieces, q % 2) for q in range(pieces)]

    def rows_of(sub):
        return pl.ds(pl.multiple_of(sub * rows, rows), rows)

    local = pltpu.make_async_copy(r_ref, g.at[z, rows_of(s)], local_sem.at[0])
    local.start()
    barrier = pltpu.get_barrier_semaphore()

    def greet(o, carry):
        t = lax.rem(me + o, peers)
        pl.semaphore_signal(
            barrier, inc=1, device_id={"chan": t // 2, "sub": t % 2}, device_id_type=MESH
        )
        return carry

    lax.fori_loop(1, peers, greet, 0)
    for o in range(1, wins):
        pl.semaphore_signal(
            barrier, inc=1, device_id={"win": lax.rem(w + o, wins)}, device_id_type=MESH
        )
    local.wait()
    moments = lax.dot_general(
        p_ref[...], g[z, rows_of(s), :], (((1,), (0,)), ((), ())),
        preferred_element_type=jnp.float32,
    )
    for q in range(pieces):
        zl[q] = moments[q * PIECE : (q + 1) * PIECE, :].astype(zl.dtype)
    pl.semaphore_wait(barrier, peers - 1 + wins - 1)

    def chunk_of(sub, c):
        size = rows // CHUNKS
        return pl.ds(pl.multiple_of(sub * rows + c * size, size), size)

    def to(way):
        if way == 2:
            return {"sub": other}
        return {"chan": z + (1 if way == 1 else -1)}

    def copy(j, way, c):
        place = chunk_of(s, c)
        return pltpu.make_async_remote_copy(
            src_ref=g.at[j, place],
            dst_ref=g.at[j, place],
            send_sem=r_send.at[j, way, c],
            recv_sem=r_recv.at[j, s, c],
            device_id=to(way),
            device_id_type=MESH,
        )

    def goes_down(j):
        return (z > 0) & (j >= z) & (j - z < half)

    def goes_up(j):
        return (z < chans - 1) & (j <= z) & (j + half < chans)

    def used(j):
        return lax.rem(j - z + chans, chans) < dist

    def landed(j, sub, c):
        place = chunk_of(sub, c)
        pltpu.make_async_remote_copy(
            src_ref=g.at[j, place],
            dst_ref=g.at[j, place],
            send_sem=r_send.at[j, 2, c],
            recv_sem=r_recv.at[j, sub, c],
            device_id={"sub": other},
            device_id_type=MESH,
        ).wait_recv()

    def piece_copy(q):
        return pltpu.make_async_remote_copy(
            src_ref=zl.at[q],
            dst_ref=zr.at[me],
            send_sem=z_send.at[q],
            recv_sem=z_recv.at[me],
            device_id={"chan": owners[q][0], "sub": owners[q][1]},
            device_id_type=MESH,
        )

    def owns(q):
        return (z == owners[q][0]) & (s == owners[q][1])

    def peer(o):
        t = lax.rem(me + o, peers)
        return t, {"chan": t // 2, "sub": t % 2}

    def piece_landed(o, carry):
        t, device = peer(o)
        pltpu.make_async_remote_copy(
            src_ref=zr.at[t],
            dst_ref=zr.at[t],
            send_sem=z_send.at[0],
            recv_sem=z_recv.at[t],
            device_id=device,
            device_id_type=MESH,
        ).wait_recv()
        return carry

    def sum_copy(q, o):
        t, device = peer(o)
        return pltpu.make_async_remote_copy(
            src_ref=zs.at[q],
            dst_ref=zs.at[q],
            send_sem=y_send.at[t],
            recv_sem=y_recv.at[q],
            device_id=device,
            device_id_type=MESH,
        )

    def halo(up):
        source = pl.ds(width - LANES, LANES) if up else pl.ds(0, LANES)
        target = pl.ds(0, LANES) if up else pl.ds(width + LANES, LANES)
        return pltpu.make_async_remote_copy(
            src_ref=g.at[z, rows_of(s), source],
            dst_ref=ext.at[:, target],
            send_sem=h_send.at[int(up)],
            recv_sem=h_recv.at[int(up)],
            device_id={"win": w + (1 if up else -1)},
            device_id_type=MESH,
        )

    @pl.when(w < wins - 1)
    def _():
        halo(True).start()

    @pl.when(w > 0)
    def _():
        halo(False).start()

    for q in range(pieces):

        @pl.when(jnp.logical_not(owns(q)))
        def _(q=q):
            piece_copy(q).start()

    for c in range(CHUNKS):

        @pl.when(goes_up(z))
        def _(c=c):
            copy(z, 1, c).start()

        @pl.when(goes_down(z))
        def _(c=c):
            copy(z, 0, c).start()

    for c in range(CHUNKS):
        copy(z, 2, c).start()

    @pl.when(w == 0)
    def _():
        ext[:, :LANES] = jnp.zeros((rows, LANES), ext.dtype)

    @pl.when(w == wins - 1)
    def _():
        ext[:, LANES + width :] = jnp.zeros((rows, LANES), ext.dtype)

    ext[:, LANES : LANES + width] = g[z, rows_of(s), :]
    band_high, band_low = halves(banded(w_ref[...]))

    @pl.when(w > 0)
    def _():
        halo(True).wait_recv()

    @pl.when(w < wins - 1)
    def _():
        halo(False).wait_recv()

    for b in range(width // LANES):
        window = ext[:, b * LANES : (b + 3) * LANES]
        value = dot_rows(window, band_high) + dot_rows(window, band_low)
        high, low = halves(value)
        filt[0, :, b * LANES : (b + 1) * LANES] = high
        filt[1, :, b * LANES : (b + 1) * LANES] = low

    for q in range(pieces):

        @pl.when(owns(q))
        def _(q=q):
            lax.fori_loop(1, peers, piece_landed, 0)
            zr[me] = zl[q]
            total = lax.fori_loop(
                1, peers, lambda t, run: run + zr[t].astype(jnp.float32),
                zr[0].astype(jnp.float32),
            )
            zs[q] = total.astype(zs.dtype)

            def send(o, carry):
                sum_copy(q, o).start()
                return carry

            lax.fori_loop(1, peers, send, 0)

    def part_copy(d, o):
        t = lax.rem(w + o, wins)
        return pltpu.make_async_remote_copy(
            src_ref=sendp.at[d, t],
            dst_ref=recvp.at[d, w],
            send_sem=c_send.at[d, t],
            recv_sem=c_recv.at[d, w],
            device_id={"win": t},
            device_id_type=MESH,
        )

    def block(j):
        value = dot_rows(filt[0], g[j]) + dot_rows(filt[1], g[j])
        d = lax.rem(j - z + chans, chans)
        for t in range(wins):
            piece = value[:, t * part_width : (t + 1) * part_width]
            part[d, t] = piece
            sendp[d, t] = piece.astype(sendp.dtype)
        for o in range(1, wins):
            part_copy(d, o).start()

    def forward_chunk(h, c):
        above, below = z + h, z - h

        @pl.when((above < chans) & (h <= half))
        def _():
            landed(above, s, c)

            @pl.when(goes_down(above))
            def _():
                copy(above, 0, c).start()

            copy(above, 2, c).start()

        @pl.when((below >= 0) & (below + half < chans))
        def _():
            landed(below, s, c)

            @pl.when(goes_up(below))
            def _():
                copy(below, 1, c).start()

            @pl.when(used(below))
            def _():
                copy(below, 2, c).start()

    def forward(h):
        for c in range(CHUNKS):
            forward_chunk(h, c)

    def take(h):
        above, below = z + h, z - h

        @pl.when((above < chans) & (h <= half))
        def _():
            for c in range(CHUNKS):
                landed(above, other, c)
            block(above)

        @pl.when((below >= 0) & (below + half < chans) & (h >= half))
        def _():
            for c in range(CHUNKS):
                landed(below, other, c)
            block(below)

    forward(1)
    for q in range(pieces):

        @pl.when(jnp.logical_not(owns(q)))
        def _(q=q):
            sum_copy(q, 1).wait_recv()

    moments = zs[...].reshape(pieces * PIECE, width)
    ib[w] = dot_rows(moments, filt[0]) + dot_rows(moments, filt[1])

    def image_copy(o):
        t = lax.rem(w + o, wins)
        return pltpu.make_async_remote_copy(
            src_ref=ib.at[w],
            dst_ref=ib.at[w],
            send_sem=i_send.at[t],
            recv_sem=i_recv.at[w],
            device_id={"win": t},
            device_id_type=MESH,
        )

    def image_landed(o):
        t = lax.rem(w + o, wins)
        return pltpu.make_async_remote_copy(
            src_ref=ib.at[t],
            dst_ref=ib.at[t],
            send_sem=i_send.at[t],
            recv_sem=i_recv.at[t],
            device_id={"win": t},
            device_id_type=MESH,
        )

    for o in range(1, wins):
        image_copy(o).start()
    for c in range(CHUNKS):
        landed(z, other, c)
    block(z)
    take(1)
    for o in range(1, wins):
        image_landed(o).wait_recv()
    images = ib[0]
    for t in range(1, wins):
        images = images + ib[t]
    images = images * (1.0 / samples)
    gram = dot_rows(images, images, HIGHEST)
    k = gram.shape[0]
    gb[me] = jnp.concatenate([gram[: k // 2], gram[k // 2 :]], axis=1)

    def gram_copy(o, slot):
        t = lax.rem(me + o, peers)
        at = t if slot else me
        return pltpu.make_async_remote_copy(
            src_ref=gb.at[at],
            dst_ref=gb.at[at],
            send_sem=g_send.at[t],
            recv_sem=g_recv.at[at],
            device_id={"chan": t // 2, "sub": t % 2},
            device_id_type=MESH,
        )

    def gram_start(o, carry):
        gram_copy(o, False).start()
        return carry

    lax.fori_loop(1, peers, gram_start, 0)

    def hop(h, carry):
        forward(h)
        take(h)
        return carry

    lax.fori_loop(2, chans, hop, 0)

    def gram_landed(o, carry):
        gram_copy(o, True).wait_recv()
        return carry

    lax.fori_loop(1, peers, gram_landed, 0)
    gram = lax.fori_loop(1, peers, lambda t, total: total + gb[t], gb[0])
    gram = jnp.concatenate([gram[:, :k], gram[:, k:]], axis=0)
    inverse = inverse_factor(gram * (1.0 / (rows * peers)))
    sub_ref[...] = jnp.dot(inverse, images, precision=HIGHEST)

    def finish(d, carry):
        total = part[d, w]
        for o in range(1, wins):
            t = lax.rem(w + o, wins)
            pltpu.make_async_remote_copy(
                src_ref=recvp.at[d, t],
                dst_ref=recvp.at[d, t],
                send_sem=c_send.at[d, t],
                recv_sem=c_recv.at[d, t],
                device_id={"win": t},
                device_id_type=MESH,
            ).wait_recv()
            total = total + recvp[d, t].astype(jnp.float32)
        cov_ref[d] = (total * (1.0 / samples)).astype(cov_ref.dtype)
        return carry

    lax.fori_loop(0, dist, finish, 0)

    @pl.when(w < wins - 1)
    def _():
        halo(True).wait_send()

    @pl.when(w > 0)
    def _():
        halo(False).wait_send()

    for q in range(pieces):

        @pl.when(jnp.logical_not(owns(q)))
        def _(q=q):
            piece_copy(q).wait_send()

        @pl.when(owns(q))
        def _(q=q):
            def sent(o, carry):
                sum_copy(q, o).wait_send()
                return carry

            lax.fori_loop(1, peers, sent, 0)

    def drain(j, carry):
        for c in range(CHUNKS):

            @pl.when(goes_down(j))
            def _(c=c):
                copy(j, 0, c).wait_send()

            @pl.when(goes_up(j))
            def _(c=c):
                copy(j, 1, c).wait_send()

            @pl.when(used(j))
            def _(c=c):
                copy(j, 2, c).wait_send()

        return carry

    lax.fori_loop(0, chans, drain, 0)

    def drain_parts(d, carry):
        for o in range(1, wins):
            part_copy(d, o).wait_send()
        return carry

    lax.fori_loop(0, dist, drain_parts, 0)
    for o in range(1, wins):
        image_copy(o).wait_send()

    def drain_gram(o, carry):
        gram_copy(o, False).wait_send()
        return carry

    lax.fori_loop(1, peers, drain_gram, 0)


def body(chans, wins, records, lag_weights, probes):
    rows, width = records.shape
    k = probes.shape[1]
    dist = chans // 2 + 1
    part_width = 2 * rows // wins
    dma = pltpu.SemaphoreType.DMA
    covariance, transposed = pl.pallas_call(
        functools.partial(kernel, chans, wins, width * wins),
        out_shape=(
            jax.ShapeDtypeStruct((dist, rows, part_width), jnp.bfloat16),
            jax.ShapeDtypeStruct((k, rows), jnp.float32),
        ),
        in_specs=[
            pl.BlockSpec(memory_space=pltpu.HBM),
            pl.BlockSpec(memory_space=pltpu.VMEM),
            pl.BlockSpec(memory_space=pltpu.VMEM),
        ],
        out_specs=(pl.BlockSpec(memory_space=pltpu.VMEM),) * 2,
        scratch_shapes=[
            pltpu.VMEM((chans, 2 * rows, width), jnp.bfloat16),
            pltpu.VMEM((rows, width + 2 * LANES), jnp.bfloat16),
            pltpu.VMEM((2, rows, width), jnp.bfloat16),
            pltpu.VMEM((dist, wins, rows, part_width), jnp.float32),
            pltpu.VMEM((dist, wins, rows, part_width), jnp.bfloat16),
            pltpu.VMEM((dist, wins, rows, part_width), jnp.bfloat16),
            pltpu.VMEM((k // PIECE, PIECE, width), jnp.bfloat16),
            pltpu.VMEM((2 * chans, PIECE, width), jnp.bfloat16),
            pltpu.VMEM((k // PIECE, PIECE, width), jnp.bfloat16),
            pltpu.VMEM((wins, k, rows), jnp.float32),
            pltpu.VMEM((2 * chans, k // 2, 2 * k), jnp.float32),
            dma((1,)),
            dma((chans, 3, CHUNKS)), dma((chans, 2, CHUNKS)),
            dma((k // PIECE,)), dma((2 * chans,)),
            dma((2 * chans,)), dma((k // PIECE,)),
            dma((2,)), dma((2,)),
            dma((dist, wins)), dma((dist, wins)),
            dma((wins,)), dma((wins,)),
            dma((2 * chans,)), dma((2 * chans,)),
        ],
        compiler_params=pltpu.CompilerParams(
            collective_id=0, has_side_effects=True, vmem_limit_bytes=48 * 1024 * 1024
        ),
    )(records, lag_weights.reshape(1, -1), probes.T)
    return covariance, transposed.T


def solution(mesh):
    return jax.shard_map(
        functools.partial(body, mesh.shape["chan"], mesh.shape["win"]),
        mesh=mesh,
        in_specs=(P(("groups", "chan", "sub"), "win"), P(), P(("groups", "chan", "sub"), None)),
        out_specs=(P(None, ("groups", "chan", "sub"), "win"), P(("groups", "chan", "sub"), None)),
        check_vma=False,
    )
```

```python
import functools

import jax
import jax.numpy as jnp
from jax import lax
from jax.experimental import pallas as pl
from jax.experimental.pallas import tpu as pltpu
from jax.sharding import PartitionSpec as P

MESH = pl.DeviceIdType.MESH
MAXLAG = 32
LANES = 128
PIECE = 16
CHUNKS = 4
HIGHEST = lax.Precision.HIGHEST


def dot_rows(a, b, precision=None):
    return lax.dot_general(
        a, b, (((1,), (1,)), ((), ())), precision=precision, preferred_element_type=jnp.float32
    )


def halves(x):
    high = x.astype(jnp.bfloat16)
    return high, (x - high.astype(jnp.float32)).astype(jnp.bfloat16)


def banded(weights):
    count = weights.shape[1]
    start = LANES - MAXLAG
    lag = lax.broadcasted_iota(jnp.int32, (count, 3 * LANES), 0)
    place = lax.broadcasted_iota(jnp.int32, (count, 3 * LANES), 1)
    forward = jnp.where(place == lag + start, 0.5, 0.0)
    backward = jnp.where(place == start + count - 1 - lag, 0.5, 0.0)
    row = jnp.dot(weights, forward + backward, precision=HIGHEST)
    row = jnp.broadcast_to(row, (LANES, 3 * LANES))
    return pltpu.roll(row, 0, 1, stride=1, stride_axis=0)


def inverse_factor(gram):
    k = gram.shape[0]
    rows = lax.broadcasted_iota(jnp.int32, (k, k), 0)
    columns = lax.broadcasted_iota(jnp.int32, (k, k), 1)
    eye = jnp.where(rows == columns, 1.0, 0.0)
    m = jnp.concatenate([gram, eye], axis=1)
    below = lax.broadcasted_iota(jnp.int32, (k, 1), 0)
    for i in range(k - 1):
        column = m[:, i : i + 1]
        factor = jnp.where(below > i, column / m[i : i + 1, i : i + 1], 0.0)
        m = m - factor * m[i : i + 1, :]
    pivots = jnp.sum(m[:, :k] * eye, axis=1, keepdims=True)
    return m[:, k:] / jnp.sqrt(pivots)


def kernel(
    chans, wins, samples,
    r_ref, w_ref, p_ref,
    cov_ref, sub_ref,
    g, ext, filt, part, sendp, recvp, zl, zr, zs, ib, gb,
    local_sem, r_send, r_recv, z_send, z_recv, y_send, y_recv, h_send, h_recv,
    c_send, c_recv, i_send, i_recv, g_send, g_recv,
):
    z = lax.axis_index("chan")
    s = lax.axis_index("sub")
    w = lax.axis_index("win")
    rows, width = r_ref.shape
    dist = cov_ref.shape[0]
    part_width = cov_ref.shape[2]
    peers = 2 * chans
    me = z * 2 + s
    other = 1 - s
    half = chans // 2
    pieces = zs.shape[0]
    owners = [((q * chans) // pieces, q % 2) for q in range(pieces)]

    def rows_of(sub):
        return pl.ds(pl.multiple_of(sub * rows, rows), rows)

    local = pltpu.make_async_copy(r_ref, g.at[z, rows_of(s)], local_sem.at[0])
    local.start()
    barrier = pltpu.get_barrier_semaphore()

    def greet(o, carry):
        t = lax.rem(me + o, peers)
        pl.semaphore_signal(
            barrier, inc=1, device_id={"chan": t // 2, "sub": t % 2}, device_id_type=MESH
        )
        return carry

    lax.fori_loop(1, peers, greet, 0)
    for o in range(1, wins):
        pl.semaphore_signal(
            barrier, inc=1, device_id={"win": lax.rem(w + o, wins)}, device_id_type=MESH
        )
    local.wait()
    moments = lax.dot_general(
        p_ref[...], g[z, rows_of(s), :], (((1,), (0,)), ((), ())),
        preferred_element_type=jnp.float32,
    )
    for q in range(pieces):
        zl[q] = moments[q * PIECE : (q + 1) * PIECE, :].astype(zl.dtype)
    pl.semaphore_wait(barrier, peers - 1 + wins - 1)

    def chunk_of(sub, c):
        size = rows // CHUNKS
        return pl.ds(pl.multiple_of(sub * rows + c * size, size), size)

    def to(way):
        if way == 2:
            return {"sub": other}
        return {"chan": z + (1 if way == 1 else -1)}

    def copy(j, way, c):
        place = chunk_of(s, c)
        return pltpu.make_async_remote_copy(
            src_ref=g.at[j, place],
            dst_ref=g.at[j, place],
            send_sem=r_send.at[j, way, c],
            recv_sem=r_recv.at[j, s, c],
            device_id=to(way),
            device_id_type=MESH,
        )

    def goes_down(j):
        return (z > 0) & (j >= z) & (j - z < half)

    def goes_up(j):
        return (z < chans - 1) & (j <= z) & (j + half < chans)

    def used(j):
        return lax.rem(j - z + chans, chans) < dist

    def landed(j, sub, c):
        place = chunk_of(sub, c)
        pltpu.make_async_remote_copy(
            src_ref=g.at[j, place],
            dst_ref=g.at[j, place],
            send_sem=r_send.at[j, 2, c],
            recv_sem=r_recv.at[j, sub, c],
            device_id={"sub": other},
            device_id_type=MESH,
        ).wait_recv()

    def piece_copy(q):
        return pltpu.make_async_remote_copy(
            src_ref=zl.at[q],
            dst_ref=zr.at[me],
            send_sem=z_send.at[q],
            recv_sem=z_recv.at[me],
            device_id={"chan": owners[q][0], "sub": owners[q][1]},
            device_id_type=MESH,
        )

    def owns(q):
        return (z == owners[q][0]) & (s == owners[q][1])

    def peer(o):
        t = lax.rem(me + o, peers)
        return t, {"chan": t // 2, "sub": t % 2}

    def piece_landed(o, carry):
        t, device = peer(o)
        pltpu.make_async_remote_copy(
            src_ref=zr.at[t],
            dst_ref=zr.at[t],
            send_sem=z_send.at[0],
            recv_sem=z_recv.at[t],
            device_id=device,
            device_id_type=MESH,
        ).wait_recv()
        return carry

    def sum_copy(q, o):
        t, device = peer(o)
        return pltpu.make_async_remote_copy(
            src_ref=zs.at[q],
            dst_ref=zs.at[q],
            send_sem=y_send.at[t],
            recv_sem=y_recv.at[q],
            device_id=device,
            device_id_type=MESH,
        )

    def halo(up):
        source = pl.ds(width - LANES, LANES) if up else pl.ds(0, LANES)
        target = pl.ds(0, LANES) if up else pl.ds(width + LANES, LANES)
        return pltpu.make_async_remote_copy(
            src_ref=g.at[z, rows_of(s), source],
            dst_ref=ext.at[:, target],
            send_sem=h_send.at[int(up)],
            recv_sem=h_recv.at[int(up)],
            device_id={"win": w + (1 if up else -1)},
            device_id_type=MESH,
        )

    @pl.when(w < wins - 1)
    def _():
        halo(True).start()

    @pl.when(w > 0)
    def _():
        halo(False).start()

    for q in range(pieces):

        @pl.when(jnp.logical_not(owns(q)))
        def _(q=q):
            piece_copy(q).start()

    for c in range(CHUNKS):

        @pl.when(goes_up(z))
        def _(c=c):
            copy(z, 1, c).start()

        @pl.when(goes_down(z))
        def _(c=c):
            copy(z, 0, c).start()

    for c in range(CHUNKS):
        copy(z, 2, c).start()

    @pl.when(w == 0)
    def _():
        ext[:, :LANES] = jnp.zeros((rows, LANES), ext.dtype)

    @pl.when(w == wins - 1)
    def _():
        ext[:, LANES + width :] = jnp.zeros((rows, LANES), ext.dtype)

    ext[:, LANES : LANES + width] = g[z, rows_of(s), :]
    band_high, band_low = halves(banded(w_ref[...]))

    @pl.when(w > 0)
    def _():
        halo(True).wait_recv()

    @pl.when(w < wins - 1)
    def _():
        halo(False).wait_recv()

    for b in range(width // LANES):
        window = ext[:, b * LANES : (b + 3) * LANES]
        value = dot_rows(window, band_high) + dot_rows(window, band_low)
        high, low = halves(value)
        filt[0, :, b * LANES : (b + 1) * LANES] = high
        filt[1, :, b * LANES : (b + 1) * LANES] = low

    for q in range(pieces):

        @pl.when(owns(q))
        def _(q=q):
            lax.fori_loop(1, peers, piece_landed, 0)
            zr[me] = zl[q]
            total = lax.fori_loop(
                1, peers, lambda t, run: run + zr[t].astype(jnp.float32),
                zr[0].astype(jnp.float32),
            )
            zs[q] = total.astype(zs.dtype)

            def send(o, carry):
                sum_copy(q, o).start()
                return carry

            lax.fori_loop(1, peers, send, 0)

    def part_copy(d, o):
        t = lax.rem(w + o, wins)
        return pltpu.make_async_remote_copy(
            src_ref=sendp.at[d, t],
            dst_ref=recvp.at[d, w],
            send_sem=c_send.at[d, t],
            recv_sem=c_recv.at[d, w],
            device_id={"win": t},
            device_id_type=MESH,
        )

    def block(j):
        value = dot_rows(filt[0], g[j]) + dot_rows(filt[1], g[j])
        d = lax.rem(j - z + chans, chans)
        for t in range(wins):
            piece = value[:, t * part_width : (t + 1) * part_width]
            part[d, t] = piece
            sendp[d, t] = piece.astype(sendp.dtype)
        for o in range(1, wins):
            part_copy(d, o).start()

    def forward_chunk(h, c):
        above, below = z + h, z - h

        @pl.when((above < chans) & (h <= half))
        def _():
            landed(above, s, c)

            @pl.when(goes_down(above))
            def _():
                copy(above, 0, c).start()

            copy(above, 2, c).start()

        @pl.when((below >= 0) & (below + half < chans))
        def _():
            landed(below, s, c)

            @pl.when(goes_up(below))
            def _():
                copy(below, 1, c).start()

            @pl.when(used(below))
            def _():
                copy(below, 2, c).start()

    def forward(h):
        for c in range(CHUNKS):
            forward_chunk(h, c)

    def take(h):
        above, below = z + h, z - h

        @pl.when((above < chans) & (h <= half))
        def _():
            for c in range(CHUNKS):
                landed(above, other, c)
            block(above)

        @pl.when((below >= 0) & (below + half < chans) & (h >= half))
        def _():
            for c in range(CHUNKS):
                landed(below, other, c)
            block(below)

    forward(1)
    for q in range(pieces):

        @pl.when(jnp.logical_not(owns(q)))
        def _(q=q):
            sum_copy(q, 1).wait_recv()

    moments = zs[...].reshape(pieces * PIECE, width)
    ib[w] = dot_rows(moments, filt[0]) + dot_rows(moments, filt[1])

    def image_copy(o):
        t = lax.rem(w + o, wins)
        return pltpu.make_async_remote_copy(
            src_ref=ib.at[w],
            dst_ref=ib.at[w],
            send_sem=i_send.at[t],
            recv_sem=i_recv.at[w],
            device_id={"win": t},
            device_id_type=MESH,
        )

    def image_landed(o):
        t = lax.rem(w + o, wins)
        return pltpu.make_async_remote_copy(
            src_ref=ib.at[t],
            dst_ref=ib.at[t],
            send_sem=i_send.at[t],
            recv_sem=i_recv.at[t],
            device_id={"win": t},
            device_id_type=MESH,
        )

    for o in range(1, wins):
        image_copy(o).start()
    for c in range(CHUNKS):
        landed(z, other, c)
    block(z)
    take(1)
    if chans > 2:
        forward(2)
    for o in range(1, wins):
        image_landed(o).wait_recv()
    images = ib[0]
    for t in range(1, wins):
        images = images + ib[t]
    images = images * (1.0 / samples)
    gram = dot_rows(images, images, HIGHEST)
    k = gram.shape[0]
    gb[me] = jnp.concatenate([gram[: k // 2], gram[k // 2 :]], axis=1)

    def gram_copy(o, slot):
        t = lax.rem(me + o, peers)
        at = t if slot else me
        return pltpu.make_async_remote_copy(
            src_ref=gb.at[at],
            dst_ref=gb.at[at],
            send_sem=g_send.at[t],
            recv_sem=g_recv.at[at],
            device_id={"chan": t // 2, "sub": t % 2},
            device_id_type=MESH,
        )

    def gram_start(o, carry):
        gram_copy(o, False).start()
        return carry

    lax.fori_loop(1, peers, gram_start, 0)

    def hop(h, carry):
        forward(h)
        take(h)
        return carry

    if chans > 2:
        take(2)
    lax.fori_loop(3, chans, hop, 0)

    def gram_landed(o, carry):
        gram_copy(o, True).wait_recv()
        return carry

    lax.fori_loop(1, peers, gram_landed, 0)
    gram = lax.fori_loop(1, peers, lambda t, total: total + gb[t], gb[0])
    gram = jnp.concatenate([gram[:, :k], gram[:, k:]], axis=0)
    inverse = inverse_factor(gram * (1.0 / (rows * peers)))
    sub_ref[...] = jnp.dot(inverse, images, precision=HIGHEST)

    def finish(d, carry):
        total = part[d, w]
        for o in range(1, wins):
            t = lax.rem(w + o, wins)
            pltpu.make_async_remote_copy(
                src_ref=recvp.at[d, t],
                dst_ref=recvp.at[d, t],
                send_sem=c_send.at[d, t],
                recv_sem=c_recv.at[d, t],
                device_id={"win": t},
                device_id_type=MESH,
            ).wait_recv()
            total = total + recvp[d, t].astype(jnp.float32)
        cov_ref[d] = (total * (1.0 / samples)).astype(cov_ref.dtype)
        return carry

    lax.fori_loop(0, dist, finish, 0)

    @pl.when(w < wins - 1)
    def _():
        halo(True).wait_send()

    @pl.when(w > 0)
    def _():
        halo(False).wait_send()

    for q in range(pieces):

        @pl.when(jnp.logical_not(owns(q)))
        def _(q=q):
            piece_copy(q).wait_send()

        @pl.when(owns(q))
        def _(q=q):
            def sent(o, carry):
                sum_copy(q, o).wait_send()
                return carry

            lax.fori_loop(1, peers, sent, 0)

    def drain(j, carry):
        for c in range(CHUNKS):

            @pl.when(goes_down(j))
            def _(c=c):
                copy(j, 0, c).wait_send()

            @pl.when(goes_up(j))
            def _(c=c):
                copy(j, 1, c).wait_send()

            @pl.when(used(j))
            def _(c=c):
                copy(j, 2, c).wait_send()

        return carry

    lax.fori_loop(0, chans, drain, 0)

    def drain_parts(d, carry):
        for o in range(1, wins):
            part_copy(d, o).wait_send()
        return carry

    lax.fori_loop(0, dist, drain_parts, 0)
    for o in range(1, wins):
        image_copy(o).wait_send()

    def drain_gram(o, carry):
        gram_copy(o, False).wait_send()
        return carry

    lax.fori_loop(1, peers, drain_gram, 0)


def body(chans, wins, records, lag_weights, probes):
    rows, width = records.shape
    k = probes.shape[1]
    dist = chans // 2 + 1
    part_width = 2 * rows // wins
    dma = pltpu.SemaphoreType.DMA
    covariance, transposed = pl.pallas_call(
        functools.partial(kernel, chans, wins, width * wins),
        out_shape=(
            jax.ShapeDtypeStruct((dist, rows, part_width), jnp.bfloat16),
            jax.ShapeDtypeStruct((k, rows), jnp.float32),
        ),
        in_specs=[
            pl.BlockSpec(memory_space=pltpu.HBM),
            pl.BlockSpec(memory_space=pltpu.VMEM),
            pl.BlockSpec(memory_space=pltpu.VMEM),
        ],
        out_specs=(pl.BlockSpec(memory_space=pltpu.VMEM),) * 2,
        scratch_shapes=[
            pltpu.VMEM((chans, 2 * rows, width), jnp.bfloat16),
            pltpu.VMEM((rows, width + 2 * LANES), jnp.bfloat16),
            pltpu.VMEM((2, rows, width), jnp.bfloat16),
            pltpu.VMEM((dist, wins, rows, part_width), jnp.float32),
            pltpu.VMEM((dist, wins, rows, part_width), jnp.bfloat16),
            pltpu.VMEM((dist, wins, rows, part_width), jnp.bfloat16),
            pltpu.VMEM((k // PIECE, PIECE, width), jnp.bfloat16),
            pltpu.VMEM((2 * chans, PIECE, width), jnp.bfloat16),
            pltpu.VMEM((k // PIECE, PIECE, width), jnp.bfloat16),
            pltpu.VMEM((wins, k, rows), jnp.float32),
            pltpu.VMEM((2 * chans, k // 2, 2 * k), jnp.float32),
            dma((1,)),
            dma((chans, 3, CHUNKS)), dma((chans, 2, CHUNKS)),
            dma((k // PIECE,)), dma((2 * chans,)),
            dma((2 * chans,)), dma((k // PIECE,)),
            dma((2,)), dma((2,)),
            dma((dist, wins)), dma((dist, wins)),
            dma((wins,)), dma((wins,)),
            dma((2 * chans,)), dma((2 * chans,)),
        ],
        compiler_params=pltpu.CompilerParams(
            collective_id=0, has_side_effects=True, vmem_limit_bytes=48 * 1024 * 1024
        ),
    )(records, lag_weights.reshape(1, -1), probes.T)
    return covariance, transposed.T


def solution(mesh):
    return jax.shard_map(
        functools.partial(body, mesh.shape["chan"], mesh.shape["win"]),
        mesh=mesh,
        in_specs=(P(("groups", "chan", "sub"), "win"), P(), P(("groups", "chan", "sub"), None)),
        out_specs=(P(None, ("groups", "chan", "sub"), "win"), P(("groups", "chan", "sub"), None)),
        check_vma=False,
    )
```
